32 devices in a mesh: dp: 8 (over z, y), mp: 4 (over x, core).
Axes of the slice: x: 2, y: 2, z: 4, core: 2. Of those that a mesh axis runs over, the one named last changes fastest.
Arguments:
- features: bfloat16 [32768, 1024], P('dp', 'mp'), may hold values from -6 to 6
- history: bfloat16 [16384, 1024], P('dp', 'mp'), may hold values from -6 to 6
- adj_values: bfloat16 [256, 8, 128, 128], P('dp'), may hold values from -0.1875 to 0.1875
- adj_sources: int32 [256, 8], P('dp'), may hold values from 0 to 79, as said below
- pull_list: int32 [8, 8, 2], P('dp'), may hold values from 0 to 15
- pull_count: int32 [8, 8], P('dp'), may hold values from 0 to 2, as said below
- partner_mask: int32 [1], replicated, may hold values from 1 to 7
- weight: bfloat16 [1024, 1024], P('mp'), may hold values from -0.1875 to 0.1875
- bias: float32 [1024], P('mp'), may hold values from -3 to 3
Outputs:
- layer_out: bfloat16 [32768, 1024], P('dp', 'mp')
The draws below stay inside these ranges and needn't reach their ends.
Inputs may be any that keep to these rules, and one draw needn't show every extreme that they name: The partner of cluster c is cluster c XOR partner_mask[0]. Slots s >= pull_count[c, o] of pull_list[c, o] are not live; in every draw some owner has all 2 slots live for every cluster. `adj_sources`: indexes sources: own blocks, then partner blocks, then pulled slots; tile 0 of every target block names an own block and tile 1 a partner block. `pull_list`: local block numbers within an owner's history.
All inputs are finite; a program needn't handle non-finite values.
Results may differ from the reference program's by a relative error of at most 0.0045.
Values may be sent and summed in bfloat16 or wider, within the bound.
No kernel may reach another device: no remote copies, remote signals or barrier semaphores. Data moves between devices by JAX's collectives and lax.ppermute only.
A program may use at most 128 MiB of HBM per device.

```python
import jax
import jax.numpy as jnp
from jax import lax

D = 1024
RB = 32
KB = 8
CAP = 2
HBLK = 16
NODES = 32768
HNODES = 16384
NSRC = 80
N_DP = 8


def draw_pull_count(key, part):
    base_counts = jax.random.randint(key, (N_DP, N_DP), 0, CAP + 1)
    hot_owner = jax.random.randint(jax.random.fold_in(key, 7), (), 0, N_DP)
    column_ids = jnp.arange(N_DP, dtype=jnp.int32)
    filled = jnp.where((column_ids == hot_owner)[None, :], CAP, base_counts)
    return filled.astype(jnp.int32)


def draw_adj_sources(key, part):
    total_rows = N_DP * RB
    spread_src = jax.random.randint(jax.random.fold_in(key, 11), (total_rows, KB), 0, NSRC)
    own_src = jax.random.randint(jax.random.fold_in(key, 12), (total_rows, KB), 0, RB)
    partner_src = RB + jax.random.randint(jax.random.fold_in(key, 13), (total_rows, KB), 0, RB)
    tile_ids = jnp.arange(KB, dtype=jnp.int32)[None, :]
    row_ids = jnp.arange(total_rows, dtype=jnp.int32)[:, None]
    chosen = jnp.where(tile_ids == 0, own_src, jnp.where(tile_ids == 1, partner_src, spread_src))
    chosen = jnp.where((row_ids == 0) & (tile_ids == KB - 1), NSRC - 1, chosen)
    return chosen.astype(jnp.int32)


def plant(entries, own_key, smallest, top_value):
    longest = entries.shape.index(max(entries.shape))
    spots = []
    for shift in (0, 1):
        where = [jax.random.randint(jax.random.fold_in(own_key, axis), (), 0, length) for axis, length in enumerate(entries.shape)]
        where[longest] = (where[longest] + shift) % entries.shape[longest]
        spots.append(tuple(where))
    return entries.at[spots[0]].set(smallest).at[spots[1]].set(top_value)


def block_levels(own_key, extent, pieces, smallest, top_value):
    def one(axis_at, blocks):
        draws = jax.random.uniform(jax.random.fold_in(jax.random.fold_in(own_key, 6), axis_at), (blocks,), jnp.float32, smallest / len(pieces), top_value / len(pieces))
        return jnp.repeat(jnp.exp(draws), extent[axis_at] // blocks).reshape((-1,) + (1,) * (len(extent) - axis_at - 1))

    loudness = one(*pieces[0])
    for cut in pieces[1:]:
        loudness = loudness * one(*cut)
    return loudness


def noise(rng, extent, width, limit, split=(), held_as=jnp.bfloat16):
    level = block_levels(rng, extent, split, -0.22, 0.18) if split else 1.0
    values = jax.random.normal(rng, extent, jnp.float32) * width * level
    return jnp.minimum(jnp.maximum(values, -limit), limit).astype(held_as)


def setup_inputs(seed: int = 0) -> dict:
    keys = jax.random.split(jax.random.key(seed), 10)
    return {
        "features": noise(keys[0], (NODES, D), 1.0, 6.0, ((0, 8), (1, 4))),
        "history": noise(keys[1], (HNODES, D), 1.0, 6.0, ((0, 8), (1, 4))),
        "adj_values": noise(keys[2], (N_DP * RB, KB, 128, 128), (KB * 128) ** -0.5, 0.1875, ((0, 8),)),
        "adj_sources": draw_adj_sources(jax.random.fold_in(keys[9], 71), 0),
        "pull_list": plant(jax.random.randint(keys[4], (N_DP, N_DP, CAP), 0, HBLK), jax.random.fold_in(keys[4], 1), 0, HBLK - 1).astype(jnp.int32),
        "pull_count": draw_pull_count(jax.random.fold_in(keys[9], 71), 0),
        "partner_mask": jax.random.randint(keys[6], (1,), 1, N_DP).astype(jnp.int32),
        "weight": noise(keys[7], (D, D), D ** -0.5, 0.1875, ((0, 4),)),
        "bias": noise(keys[8], (D,), 0.5, 3.0, ((0, 4),), jnp.float32),
    }


def reference(features, history, adj_values, adj_sources, pull_list, pull_count, partner_mask, weight, bias):
    row_count = RB * 128
    hist_blocks = history.reshape(N_DP * HBLK, 128, D)
    owner_ids = jnp.arange(N_DP, dtype=jnp.int32)
    slot_ids = jnp.arange(CAP, dtype=jnp.int32)

    def one_cluster(cluster):
        own_rows = lax.dynamic_slice_in_dim(features, cluster * row_count, row_count, 0)
        partner = jnp.bitwise_xor(cluster, partner_mask[0]).astype(jnp.int32)
        partner_rows = lax.dynamic_slice_in_dim(features, partner * row_count, row_count, 0)
        wanted = owner_ids[:, None] * HBLK + pull_list[cluster]
        pulled = hist_blocks[wanted]
        live_slots = slot_ids[None, :] < pull_count[cluster][:, None]
        pulled = jnp.where(live_slots[:, :, None, None], pulled, jnp.zeros((), pulled.dtype))
        sources = jnp.concatenate([own_rows.reshape(RB, 128, D), partner_rows.reshape(RB, 128, D),
                                   pulled.reshape(N_DP * CAP, 128, D)], axis=0)
        tile_values = lax.dynamic_slice_in_dim(adj_values, cluster * RB, RB, 0)
        picked_src = lax.dynamic_slice_in_dim(adj_sources, cluster * RB, RB, 0)
        gathered = sources[picked_src].astype(jnp.float32)
        agg = jnp.einsum('tkij,tkjd->tid', tile_values.astype(jnp.float32), gathered)
        agg = agg.reshape(row_count, D).astype(jnp.bfloat16)
        mixed = jnp.dot(agg, weight, preferred_element_type=jnp.float32) + bias
        return jnp.maximum(mixed, 0.0).astype(jnp.bfloat16)

    results = lax.map(one_cluster, jnp.arange(N_DP, dtype=jnp.int32))
    return results.reshape(N_DP * row_count, D)
```

```python
import functools

import jax
import jax.numpy as jnp
from jax import lax
from jax.experimental import pallas as pl
from jax.experimental.pallas import tpu as pltpu
from jax.sharding import PartitionSpec as P

BLOCK = 128
CHUNKS = 4
DIGIT_BITS = 3
VMEM = 48 * 1024 * 1024


def swap(value, axis, distance):
    pairs = [(source, source ^ distance) for source in range(lax.axis_size(axis))]
    return lax.ppermute(value, axis, pairs)


def gather_mp(value):
    parts = [value]
    bit = lax.axis_size("mp") // 2
    while bit:
        parts = parts + [swap(part, "mp", bit) for part in parts]
        bit //= 2
    return parts


def distances(count):
    order = [0]
    bit = count // 2
    while bit:
        order = order + [d ^ bit for d in order]
        bit //= 2
    return order


def mix_kernel(*refs):
    *parts, weight, out = refs
    total = jnp.dot(parts[0][...], weight[0], preferred_element_type=jnp.float32)
    for k, part in enumerate(parts[1:], 1):
        total += jnp.dot(part[...], weight[k], preferred_element_type=jnp.float32)
    out[...] = total.astype(out.dtype)


def mix(parts, weight, first_offset=0):
    rows, depth = parts[1].shape
    width = weight.shape[2]
    tile = min(512, rows)
    shift = first_offset // tile
    return pl.pallas_call(
        mix_kernel,
        grid=(rows // tile,),
        in_specs=[pl.BlockSpec((tile, depth), lambda i: (i + shift, 0))]
        + [pl.BlockSpec((tile, depth), lambda i: (i, 0))] * (len(parts) - 1)
        + [pl.BlockSpec(weight.shape, lambda i: (0, 0, 0))],
        out_specs=pl.BlockSpec((tile, width), lambda i: (i, 0)),
        out_shape=jax.ShapeDtypeStruct((rows, width), jnp.bfloat16),
        compiler_params=pltpu.CompilerParams(vmem_limit_bytes=VMEM),
        cost_estimate=pl.CostEstimate(
            flops=2 * rows * depth * width * len(parts),
            bytes_accessed=2 * rows * (depth * len(parts) + width),
            transcendentals=0,
        ),
    )(*parts, weight)


def agg_kernel(picked, adj, bias, *rest):
    *sources, out, table, sems = rest
    step = pl.program_id(0)
    targets, tiles = adj.shape[0], adj.shape[1]

    @pl.when(step == 0)
    def _():
        copies = []
        start = 0
        for i, source in enumerate(sources):
            rows = source.shape[0]
            copies.append(pltpu.make_async_copy(source, table.at[pl.ds(start, rows)], sems.at[i]))
            start += rows
        for copy in copies:
            copy.start()
        for copy in copies:
            copy.wait()

    for t in range(targets):
        lhs = jnp.concatenate([adj[t, k] for k in range(tiles)], axis=1)
        picks = []
        for k in range(tiles):
            row = pl.multiple_of(picked[step * targets + t, k] * BLOCK, BLOCK)
            picks.append(table[pl.ds(row, BLOCK), :])
        total = jnp.dot(lhs, jnp.concatenate(picks, axis=0), preferred_element_type=jnp.float32)
        out[pl.ds(t * BLOCK, BLOCK), :] = jnp.maximum(total + bias[...], 0.0).astype(out.dtype)


def aggregate(adj_sources, adj_values, bias, sources):
    target_blocks, tiles = adj_sources.shape
    width = sources[0].shape[1]
    group = 4
    total_rows = sum(s.shape[0] for s in sources)
    grid_spec = pltpu.PrefetchScalarGridSpec(
        num_scalar_prefetch=1,
        grid=(target_blocks // group,),
        in_specs=[
            pl.BlockSpec((group, tiles, BLOCK, BLOCK), lambda i, *_: (i, 0, 0, 0)),
            pl.BlockSpec((1, width), lambda i, *_: (0, 0)),
        ]
        + [pl.BlockSpec(memory_space=pl.ANY)] * len(sources),
        out_specs=pl.BlockSpec((group * BLOCK, width), lambda i, *_: (i, 0)),
        scratch_shapes=[
            pltpu.VMEM((total_rows, width), jnp.bfloat16),
            pltpu.SemaphoreType.DMA((len(sources),)),
        ],
    )
    return pl.pallas_call(
        agg_kernel,
        grid_spec=grid_spec,
        out_shape=jax.ShapeDtypeStruct((target_blocks * BLOCK, width), jnp.bfloat16),
        compiler_params=pltpu.CompilerParams(vmem_limit_bytes=VMEM),
        cost_estimate=pl.CostEstimate(
            flops=2 * target_blocks * tiles * BLOCK * BLOCK * width,
            bytes_accessed=2 * (target_blocks * tiles * BLOCK * BLOCK + total_rows * width),
            transcendentals=0,
        ),
    )(adj_sources, adj_values, bias.reshape(1, -1), *sources)


def transfers(low, features, history, pull_list, pull_count, weight):
    rows, depth = features.shape
    mp_count = lax.axis_size("mp")
    order = jnp.array(distances(mp_count), jnp.int32) ^ lax.axis_index("mp")
    columns = weight.reshape(depth, mp_count, -1).transpose(1, 0, 2)
    columns = lax.all_to_all(columns, "mp", split_axis=0, concat_axis=0, tiled=True)[order]

    wanted = lax.all_to_all(pull_list, "dp", split_axis=0, concat_axis=0, tiled=True)
    hist_blocks = history.reshape(-1, BLOCK, depth)
    pulled = lax.all_to_all(hist_blocks[wanted], "dp", split_axis=0, concat_axis=0, tiled=True)
    slots = pulled.shape[1]
    live = jnp.arange(slots, dtype=jnp.int32)[None, :] < pull_count[:, None]
    pulled = jnp.where(live[:, :, None, None], pulled, jnp.zeros((), pulled.dtype))
    pulled = pulled.reshape(-1, depth)

    step = rows // CHUNKS
    own, partner = [], []
    for start in range(0, rows, step):
        chunk = lax.slice_in_dim(features, start, start + step)
        parts = gather_mp(chunk)
        mixed = mix([features] + parts[1:], columns, start)
        own.append(mixed)
        partner.append(swap(mixed, "dp", low) if low else mixed)
    return (*own, *partner, mix(gather_mp(pulled), columns))


def per_device(
    features, history, adj_values, adj_sources, pull_list, pull_count, partner_mask, weight, bias
):
    mask = partner_mask[0]
    mask_bits = lax.axis_size("dp").bit_length() - 1
    digit_bits = min(DIGIT_BITS, mask_bits)
    branches = [functools.partial(transfers, low) for low in range(1 << digit_bits)]
    moved = lax.switch(
        mask % (1 << digit_bits),
        branches,
        features,
        history,
        pull_list[0],
        pull_count[0],
        weight,
    )
    own, partner, pulled = moved[:CHUNKS], moved[CHUNKS : 2 * CHUNKS], moved[2 * CHUNKS]
    done = digit_bits
    while done < mask_bits:
        bits = min(DIGIT_BITS, mask_bits - done)
        partner = lax.switch(
            (mask >> done) % (1 << bits),
            [lambda *p: p]
            + [
                functools.partial(lambda d, *p: tuple(swap(v, "dp", d) for v in p), digit << done)
                for digit in range(1, 1 << bits)
            ],
            *partner,
        )
        done += bits
    return aggregate(adj_sources, adj_values, bias, [*own, *partner, pulled])


def solution(mesh):
    in_specs = (
        P("dp", "mp"),
        P("dp", "mp"),
        P("dp", None, None, None),
        P("dp", None),
        P("dp", None, None),
        P("dp", None),
        P(),
        P("mp", None),
        P("mp"),
    )
    out_specs = P("dp", "mp")
    return jax.shard_map(
        per_device, mesh=mesh, in_specs=in_specs, out_specs=out_specs, check_vma=False
    )
```

```python
import functools
import math

import jax
import jax.numpy as jnp
from jax import lax
from jax.experimental import pallas as pl
from jax.experimental.pallas import tpu as pltpu
from jax.sharding import PartitionSpec as P

BLOCK = 128
RAW = 6
FIRST = 6
UNROLL = 4
CHUNKS = 2
TILE = 256
DIGIT_BITS = 3
VMEM = 48 * 1024 * 1024


def swap(value, axis, distance):
    pairs = [(source, source ^ distance) for source in range(lax.axis_size(axis))]
    return lax.ppermute(value, axis, pairs)


def swap_both(value, dp_distance, mp_distance):
    dp, mp = lax.axis_size("dp"), lax.axis_size("mp")
    pairs = [(i * mp + j, (i ^ dp_distance) * mp + (j ^ mp_distance)) for i in range(dp) for j in range(mp)]
    return lax.ppermute(value, ("dp", "mp"), pairs)


def after(value, *others):
    return lax.optimization_barrier((value, *others))[0]


def sealed(step, go, *values):
    shapes = jax.eval_shape(step, *values)
    empty = lambda *_: jax.tree.map(lambda leaf: jnp.zeros(leaf.shape, leaf.dtype), shapes)
    return lax.cond(go, step, empty, *values)


def side_of(halves, side):
    return lax.dynamic_index_in_dim(halves, (lax.axis_index("mp") % 2) ^ side, 0, keepdims=False)


def far(value):
    return [swap(value, "mp", d) for d in range(2, lax.axis_size("mp"), 2)]


def mix_kernel(_, mine, near, *refs):
    *others, weight, out, out_near = refs
    parts = [mine[0], near[...]]
    for other in others:
        parts += [other[0], other[1]]
    total = jnp.dot(parts[0], weight[0], preferred_element_type=jnp.float32)
    for k, part in enumerate(parts[1:], 1):
        total += jnp.dot(part, weight[k], preferred_element_type=jnp.float32)
    width = out.shape[1]
    out[...] = total[:, :width].astype(out.dtype)
    out_near[...] = total[:, width:].astype(out.dtype)


def mix(halves, near, others, weight, start, end, others_from=0):
    rows, depth = end - start, near.shape[1]
    width = weight.shape[2] // 2
    tile = math.gcd(TILE, math.gcd(rows, math.gcd(start, others_from)))
    shift, skip = start // tile, (start - others_from) // tile
    pair = pl.BlockSpec((2, tile, depth), lambda i, _: (0, i + skip, 0))
    grid_spec = pltpu.PrefetchScalarGridSpec(
        num_scalar_prefetch=1,
        grid=(rows // tile,),
        in_specs=[
            pl.BlockSpec((1, tile, depth), lambda i, side: (side[0], i + shift, 0)),
            pl.BlockSpec((tile, depth), lambda i, _: (i + shift, 0)),
        ]
        + [pair] * len(others)
        + [pl.BlockSpec(weight.shape, lambda i, _: (0, 0, 0))],
        out_specs=[pl.BlockSpec((tile, width), lambda i, _: (i, 0))] * 2,
    )
    return pl.pallas_call(
        mix_kernel,
        grid_spec=grid_spec,
        out_shape=[jax.ShapeDtypeStruct((rows, width), jnp.bfloat16)] * 2,
        compiler_params=pltpu.CompilerParams(vmem_limit_bytes=VMEM),
        cost_estimate=pl.CostEstimate(
            flops=2 * rows * weight.size,
            bytes_accessed=2 * rows * (weight.shape[0] * depth + 2 * width),
            transcendentals=0,
        ),
    )((lax.axis_index("mp") % 2).reshape(1), halves, near, *others, weight)


def agg_kernel(where, dead_from, picked, dead, adj, bias, *rest):
    *sources, out, table, sems = rest
    step = pl.program_id(0)
    group, tiles = adj.shape[0], adj.shape[1]

    @pl.when(step == 0)
    def _():
        copies = []
        for i, (which, start, rows, row) in enumerate(where):
            source = sources[which].at[pl.ds(start, rows)]
            copies.append(pltpu.make_async_copy(source, table.at[pl.ds(row, rows)], sems.at[i]))
        for copy in copies:
            copy.start()
        for copy in copies:
            copy.wait()

        def clear(slot, carry):
            @pl.when(dead[slot] == 1)
            def _():
                row = pl.multiple_of(dead_from + slot * BLOCK, BLOCK)
                table[pl.ds(row, BLOCK), :] = jnp.zeros((BLOCK, table.shape[1]), table.dtype)

            return carry

        lax.fori_loop(0, dead.shape[0], clear, 0)

    def some(i, _):
        for u in range(UNROLL):
            t = i * UNROLL + u
            lhs = jnp.concatenate([adj[t, k] for k in range(tiles)], axis=1)
            picks = []
            for k in range(tiles):
                row = pl.multiple_of(picked[step * group + t, k] * BLOCK, BLOCK)
                picks.append(table[pl.ds(row, BLOCK), :])
            total = jnp.dot(lhs, jnp.concatenate(picks, axis=0), preferred_element_type=jnp.float32)
            row = pl.multiple_of(t * BLOCK, BLOCK)
            out[pl.ds(row, BLOCK), :] = jnp.maximum(total + bias[...], 0.0).astype(out.dtype)
        return _

    lax.fori_loop(0, group // UNROLL, some, 0)


def aggregate(picked, dead, adj_values, bias, pieces):
    target_blocks, tiles = picked.shape
    width = bias.shape[0]
    group = math.gcd(target_blocks, 16)
    arrays, where, total_rows = [], [], 0
    for array, start, rows in pieces:
        known = [i for i, a in enumerate(arrays) if a is array]
        if not known:
            arrays.append(array)
        where.append((known[0] if known else len(arrays) - 1, start, rows, total_rows))
        total_rows += rows
    grid_spec = pltpu.PrefetchScalarGridSpec(
        num_scalar_prefetch=2,
        grid=(target_blocks // group,),
        in_specs=[
            pl.BlockSpec((group, tiles, BLOCK, BLOCK), lambda i, *_: (i, 0, 0, 0)),
            pl.BlockSpec((1, width), lambda i, *_: (0, 0)),
        ]
        + [pl.BlockSpec(memory_space=pl.ANY)] * len(arrays),
        out_specs=pl.BlockSpec((group * BLOCK, width), lambda i, *_: (i, 0)),
        scratch_shapes=[
            pltpu.VMEM((total_rows, width), jnp.bfloat16),
            pltpu.SemaphoreType.DMA((len(where),)),
        ],
    )
    return pl.pallas_call(
        functools.partial(agg_kernel, where, total_rows - dead.size * BLOCK),
        grid_spec=grid_spec,
        out_shape=jax.ShapeDtypeStruct((target_blocks * BLOCK, width), jnp.bfloat16),
        compiler_params=pltpu.CompilerParams(vmem_limit_bytes=VMEM),
        cost_estimate=pl.CostEstimate(
            flops=2 * target_blocks * tiles * BLOCK * BLOCK * width,
            bytes_accessed=2 * (target_blocks * tiles * BLOCK * BLOCK + total_rows * width),
            transcendentals=0,
        ),
    )(picked, dead, adj_values, bias.reshape(1, -1), *arrays)


def far_weight(weight):
    mp_count = lax.axis_size("mp")
    me = lax.axis_index("mp")
    width = weight.shape[1] // mp_count
    pairs = []
    for d in range(0, mp_count, 2):
        pair = [
            lax.dynamic_slice_in_dim(weight, (me ^ d ^ side) * width, width, axis=1) for side in (0, 1)
        ]
        pair = jnp.concatenate(pair, axis=1)
        pairs.append(swap(pair, "mp", d) if d else pair)
    return pairs


def all_weight(*pairs):
    depth, both = pairs[0].shape
    width = both // 2
    pairs = jnp.stack(pairs)
    flipped = jnp.concatenate([pairs[:, :, width:], pairs[:, :, :width]], axis=2)
    return jnp.stack([pairs, swap(flipped, "mp", 1)], axis=1).reshape(-1, depth, both)


def transfers(low, features, history, adj_sources, pull_list, pull_count, weight, go):
    depth = features.shape[1]
    halves = features.reshape(2, -1, depth)
    rows = halves.shape[1]
    raw_rows = rows * RAW // 16 if low >= 64 else 0
    cuts = [0, rows] if raw_rows else [0, rows * FIRST // 16, rows]
    send = list(zip(cuts[:-1], cuts[1:]))

    wanted = lax.all_to_all(pull_list, "dp", split_axis=0, concat_axis=0, tiled=True)
    weights = far_weight(weight)
    mine = side_of(halves, 0)
    near = swap(side_of(halves, 1), "mp", 1)
    raw = [swap(after(halves[:, :raw_rows], near), "dp", low)] if raw_rows else []
    sent = after(mine, *weights)
    crossed = [far(jnp.stack([sent[start:end], near[start:end]])) for start, end in send]

    def prepare(adj_sources, pull_count, *weights):
        slots = pull_list.shape[1]
        dead = (jnp.arange(slots, dtype=jnp.int32)[None, :] >= pull_count[:, None]).reshape(2, -1)
        dead = jnp.where(lax.axis_index("mp") % 2 == 1, dead[::-1], dead).reshape(-1).astype(jnp.int32)
        rows_of = places(adj_sources, features.shape[0] // BLOCK, pull_list.size)
        return all_weight(*weights), rows_of, dead

    columns, rows_of, dead = sealed(
        prepare, go, adj_sources, pull_count, after(weights[0], near), *weights[1:]
    )
    picked = history.reshape(-1, BLOCK, depth)[wanted]
    pulled = lax.all_to_all(picked, "dp", split_axis=0, concat_axis=0, tiled=True)

    own, own_near, partner, partner_near = [], [], [], []
    for start, end in send:
        parts = crossed.pop(0)
        parts[0] = after(parts[0], *raw, *own[-1:], *partner[-1:], *partner_near[-1:])
        here, beside = mix(halves, near, parts, columns, max(start, raw_rows), end, start)
        own.append(here)
        own_near.append(beside)
        partner.append(swap(here, "dp", low) if low else here)
        partner_near.append(swap_both(beside, low, 1))

    def settle(columns, foreign, own_near):
        near = swap(side_of(foreign, 1), "mp", 1)
        others = far(jnp.stack([side_of(foreign, 0), near]))
        here, beside = mix(foreign, near, others, columns, 0, near.shape[0])
        return here, [swap(value, "mp", 1) for value in [*after(own_near, *others), beside]]

    if raw:
        late, late_near = mix(halves, after(near, own[0]), parts, columns, 0, raw_rows)
        own, own_near = [late] + own, [late_near] + own_near
        first = sealed(settle, go, columns, after(raw[0], late), own_near)
        partner, partner_near = [first[0]] + partner, [first[1][-1]] + partner_near
        own_near = first[1][:-1]
    pulled = after(pulled, partner[0] if raw else own[-1])
    foreign, swapped = sealed(
        settle, go, columns, pulled.reshape(2, -1, depth), [] if raw else own_near
    )
    own_near = own_near if raw else swapped[:-1]
    tables = [*own, *own_near, *partner, *partner_near, foreign, swapped[-1]]
    pieces = [(value, 0, value.shape[0]) for value in tables]
    return rows_of, dead, pieces


def places(adj_sources, target_blocks, pulled_blocks):
    side = lax.axis_index("mp") % 2
    last = 2 * target_blocks
    pulled = last + ((adj_sources - last) ^ (side * (pulled_blocks // 2)))
    return jnp.where(adj_sources < last, adj_sources ^ (side * (target_blocks // 2)), pulled)


def layer(low, mask, features, history, adj_values, adj_sources, pull_list, pull_count, weight, bias):
    picked, dead, pieces = transfers(
        low, features, history, adj_sources, pull_list, pull_count, weight, mask > 0
    )
    mask_bits = lax.axis_size("dp").bit_length() - 1
    done = DIGIT_BITS
    if done < mask_bits:
        table = jnp.concatenate([array[start : start + rows] for array, start, rows in pieces])
        rows = features.shape[0]
        partner = table[rows : 2 * rows]
        while done < mask_bits:
            bits = min(DIGIT_BITS, mask_bits - done)
            moves = [
                functools.partial(lambda d, value: swap(value, "dp", d), digit << done)
                for digit in range(1, 1 << bits)
            ]
            partner = lax.switch((mask >> done) % (1 << bits), [lambda value: value] + moves, partner)
            done += bits
        parts = [table[:rows], partner, table[2 * rows :]]
        pieces = [(part, 0, part.shape[0]) for part in parts]
    return aggregate(picked, dead, adj_values, bias, pieces)


def per_device(
    features, history, adj_values, adj_sources, pull_list, pull_count, partner_mask, weight, bias
):
    mask = partner_mask[0]
    mask_bits = lax.axis_size("dp").bit_length() - 1
    digits = 1 << min(DIGIT_BITS, mask_bits)
    first = 1 if mask_bits <= DIGIT_BITS else 0
    return lax.switch(
        mask % digits - first,
        [functools.partial(layer, low) for low in range(first, digits)],
        mask,
        features,
        history,
        adj_values,
        adj_sources,
        pull_list[0],
        pull_count[0],
        weight,
        bias,
    )


def solution(mesh):
    in_specs = (
        P("dp", "mp"),
        P("dp", "mp"),
        P("dp", None, None, None),
        P("dp", None),
        P("dp", None, None),
        P("dp", None),
        P(),
        P("mp", None),
        P("mp"),
    )
    out_specs = P("dp", "mp")
    return jax.shard_map(
        per_device, mesh=mesh, in_specs=in_specs, out_specs=out_specs, check_vma=False
    )
```

```python
import functools
import math

import jax
import jax.numpy as jnp
from jax import lax
from jax.experimental import pallas as pl
from jax.experimental.pallas import tpu as pltpu
from jax.sharding import PartitionSpec as P

BLOCK = 128
NEAR_FIRST = 6
FAR_FIRST = 9
ROWS = 256
UNROLL = 8
CHUNKS = 2
TILE = 1024
DIGIT_BITS = 3
VMEM = 32 * 1024 * 1024


def swap(value, axis, distance):
    pairs = [(source, source ^ distance) for source in range(lax.axis_size(axis))]
    return lax.ppermute(value, axis, pairs)


def swap_both(value, dp_distance, mp_distance):
    dp, mp = lax.axis_size("dp"), lax.axis_size("mp")
    pairs = [(i * mp + j, (i ^ dp_distance) * mp + (j ^ mp_distance)) for i in range(dp) for j in range(mp)]
    return lax.ppermute(value, ("dp", "mp"), pairs)


def after(value, *others):
    return lax.optimization_barrier((value, *others))[0]


def sealed(step, go, *values):
    shapes = jax.eval_shape(step, *values)
    empty = lambda *_: jax.tree.map(lambda leaf: jnp.zeros(leaf.shape, leaf.dtype), shapes)
    return lax.cond(go, step, empty, *values)


def side_of(halves, side):
    return lax.dynamic_index_in_dim(halves, (lax.axis_index("mp") % 2) ^ side, 0, keepdims=False)


def far(value):
    return [swap(value, "mp", d) for d in range(2, lax.axis_size("mp"), 2)]


def mix_kernel(_, mine, near, *refs):
    *others, weight, out, out_near = refs
    width = out.shape[1]
    step = math.gcd(out.shape[0], ROWS)

    def some(i, carry):
        at = pl.ds(pl.multiple_of(i * step, step), step)
        parts = [mine[0, at], near[at]]
        for other in others:
            parts += [other[0, at], other[1, at]] if len(other.shape) == 3 else [other[at]]
        total = jnp.dot(parts[0], weight[0], preferred_element_type=jnp.float32)
        for k, part in enumerate(parts[1:], 1):
            total += jnp.dot(part, weight[k], preferred_element_type=jnp.float32)
        out[at] = total[:, :width].astype(out.dtype)
        out_near[at] = total[:, width:].astype(out.dtype)
        return carry

    lax.fori_loop(0, out.shape[0] // step, some, 0)


def tile_of(*counts):
    common = math.gcd(*counts)
    return max(n for n in range(BLOCK, TILE + 1, BLOCK) if common % n == 0)


def mix(halves, near, others, weight, start, end, others_from=0):
    rows, depth = end - start, near.shape[1]
    width = weight.shape[2] // 2
    tile = tile_of(rows, start, start - others_from)
    shift, skip = start // tile, (start - others_from) // tile
    pair = pl.BlockSpec((2, tile, depth), lambda i, _: (0, i + skip, 0))
    flat = pl.BlockSpec((tile, depth), lambda i, _: (i + skip, 0))
    grid_spec = pltpu.PrefetchScalarGridSpec(
        num_scalar_prefetch=1,
        grid=(rows // tile,),
        in_specs=[
            pl.BlockSpec((1, tile, depth), lambda i, side: (side[0], i + shift, 0)),
            pl.BlockSpec((tile, depth), lambda i, _: (i + shift, 0)),
        ]
        + [pair if other.ndim == 3 else flat for other in others]
        + [pl.BlockSpec(weight.shape, lambda i, _: (0, 0, 0))],
        out_specs=[pl.BlockSpec((tile, width), lambda i, _: (i, 0))] * 2,
    )
    return pl.pallas_call(
        mix_kernel,
        grid_spec=grid_spec,
        out_shape=[jax.ShapeDtypeStruct((rows, width), jnp.bfloat16)] * 2,
        compiler_params=pltpu.CompilerParams(vmem_limit_bytes=VMEM),
        cost_estimate=pl.CostEstimate(
            flops=2 * rows * weight.size,
            bytes_accessed=2 * rows * (weight.shape[0] * depth + 2 * width),
            transcendentals=0,
        ),
    )((lax.axis_index("mp") % 2).reshape(1), halves, near, *others, weight)


def agg_kernel(where, dead_from, picked, dead, adj, bias, *rest):
    *sources, out, table, sems = rest
    step = pl.program_id(0)
    group, tiles = adj.shape[0], adj.shape[1]

    @pl.when(step == 0)
    def _():
        copies = []
        for i, (which, start, rows, row) in enumerate(where):
            source = sources[which].at[pl.ds(start, rows)]
            copies.append(pltpu.make_async_copy(source, table.at[pl.ds(row, rows)], sems.at[i]))
        for copy in copies:
            copy.start()
        for copy in copies:
            copy.wait()

        def clear(slot, carry):
            @pl.when(dead[slot] == 1)
            def _():
                row = pl.multiple_of(dead_from + slot * BLOCK, BLOCK)
                table[pl.ds(row, BLOCK), :] = jnp.zeros((BLOCK, table.shape[1]), table.dtype)

            return carry

        lax.fori_loop(0, dead.shape[0], clear, 0)

    def some(i, _):
        for u in range(UNROLL):
            t = i * UNROLL + u
            lhs = jnp.concatenate([adj[t, k] for k in range(tiles)], axis=1)
            picks = []
            for k in range(tiles):
                row = pl.multiple_of(picked[step * group + t, k] * BLOCK, BLOCK)
                picks.append(table[pl.ds(row, BLOCK), :])
            total = jnp.dot(lhs, jnp.concatenate(picks, axis=0), preferred_element_type=jnp.float32)
            row = pl.multiple_of(t * BLOCK, BLOCK)
            out[pl.ds(row, BLOCK), :] = jnp.maximum(total + bias[...], 0.0).astype(out.dtype)
        return _

    lax.fori_loop(0, group // UNROLL, some, 0)


def aggregate(picked, dead, adj_values, bias, pieces):
    target_blocks, tiles = picked.shape
    width = bias.shape[0]
    group = math.gcd(target_blocks, 16)
    arrays, where, total_rows = [], [], 0
    for array, start, rows in pieces:
        known = [i for i, a in enumerate(arrays) if a is array]
        if not known:
            arrays.append(array)
        where.append((known[0] if known else len(arrays) - 1, start, rows, total_rows))
        total_rows += rows
    grid_spec = pltpu.PrefetchScalarGridSpec(
        num_scalar_prefetch=2,
        grid=(target_blocks // group,),
        in_specs=[
            pl.BlockSpec((group, tiles, BLOCK, BLOCK), lambda i, *_: (i, 0, 0, 0)),
            pl.BlockSpec((1, width), lambda i, *_: (0, 0)),
        ]
        + [pl.BlockSpec(memory_space=pl.ANY)] * len(arrays),
        out_specs=pl.BlockSpec((group * BLOCK, width), lambda i, *_: (i, 0)),
        scratch_shapes=[
            pltpu.VMEM((total_rows, width), jnp.bfloat16),
            pltpu.SemaphoreType.DMA((len(where),)),
        ],
    )
    return pl.pallas_call(
        functools.partial(agg_kernel, where, total_rows - dead.size * BLOCK),
        grid_spec=grid_spec,
        out_shape=pltpu.HBM((target_blocks * BLOCK, width), jnp.bfloat16),
        compiler_params=pltpu.CompilerParams(vmem_limit_bytes=VMEM),
        cost_estimate=pl.CostEstimate(
            flops=2 * target_blocks * tiles * BLOCK * BLOCK * width,
            bytes_accessed=2 * (target_blocks * tiles * BLOCK * BLOCK + total_rows * width),
            transcendentals=0,
        ),
    )(picked, dead, adj_values, bias.reshape(1, -1), *arrays)


def far_weight(weight):
    mp_count = lax.axis_size("mp")
    chip = lax.axis_index("mp") // 2
    both = 2 * weight.shape[1] // mp_count
    pairs = []
    for d in range(mp_count // 2):
        pair = lax.dynamic_slice_in_dim(weight, (chip ^ d) * both, both, axis=1)
        pairs.append(swap(pair, "mp", 2 * d) if d else pair)
    return pairs


def all_weight(*pairs):
    depth, both = pairs[0].shape
    width = both // 2
    pairs = jnp.stack(pairs)
    pairs = jnp.stack([pairs, swap(pairs, "mp", 1)], axis=1).reshape(-1, depth, both)
    flipped = jnp.concatenate([pairs[:, :, width:], pairs[:, :, :width]], axis=2)
    return jnp.where(lax.axis_index("mp") % 2 == 1, flipped, pairs)


def transfers(low, features, history, adj_sources, pull_list, pull_count, weight, go):
    depth = features.shape[1]
    halves = features.reshape(2, -1, depth)
    rows = halves.shape[1]
    cut = rows * (NEAR_FIRST if low < 4 else FAR_FIRST) // 16
    send = [(0, cut), (cut, rows)]

    wanted = lax.all_to_all(pull_list, "dp", split_axis=0, concat_axis=0, tiled=True)
    weights = far_weight(weight)
    mine = side_of(halves, 0)
    near = swap(side_of(halves, 1), "mp", 1)
    sent = after(mine, *weights)
    crossed = [far(jnp.stack([sent[start:end], near[start:end]])) for start, end in send]

    def prepare(adj_sources, pull_count, *weights):
        slots = pull_list.shape[1]
        dead = (jnp.arange(slots, dtype=jnp.int32)[None, :] >= pull_count[:, None]).reshape(2, -1)
        dead = jnp.where(lax.axis_index("mp") % 2 == 1, dead[::-1], dead).reshape(-1).astype(jnp.int32)
        rows_of = places(adj_sources, features.shape[0] // BLOCK, pull_list.size)
        return all_weight(*weights), rows_of, dead

    columns, rows_of, dead = sealed(
        prepare, go, adj_sources, pull_count, after(weights[0], near), *weights[1:]
    )
    picked = history.reshape(-1, BLOCK, depth)[wanted]
    pulled = lax.all_to_all(picked, "dp", split_axis=0, concat_axis=0, tiled=True)

    def to_partner(here, beside):
        return (swap(here, "dp", low) if low else here), swap_both(beside, low, 1)

    def settle(columns, foreign, *own_near):
        sent = [side_of(foreign, 0), side_of(foreign, 1)]
        near, *others = [swap(sent[d % 2], "mp", d) for d in range(1, lax.axis_size("mp"))]
        here, beside = mix(foreign, near, others, columns, 0, near.shape[0])
        return here, [swap(value, "mp", 1) for value in [*after(own_near, *others), beside]]

    first, rest = crossed
    own, beside = mix(halves, near, first, columns, 0, cut)
    moved = to_partner(own, beside)
    own_near = swap(beside, "mp", 1)
    rest[0] = after(rest[0], own, own_near)
    own_rest, beside = mix(halves, near, rest, columns, cut, rows, cut)
    if low < 4:
        moved_rest = to_partner(after(own_rest, moved[0]), after(beside, moved[1]))
    foreign = after(pulled, own_rest).reshape(2, -1, depth)
    foreign, swapped = sealed(settle, go, columns, foreign, beside)
    if low >= 4:
        moved_rest = to_partner(after(own_rest, moved[0], foreign), after(beside, moved[1], foreign))
    table = [own, own_rest, own_near, swapped[0], moved[0], moved_rest[0], moved[1], moved_rest[1]]
    pieces = [(value, 0, value.shape[0]) for value in [*table, foreign, swapped[-1]]]
    return rows_of, dead, pieces


def places(adj_sources, target_blocks, pulled_blocks):
    side = lax.axis_index("mp") % 2
    last = 2 * target_blocks
    pulled = last + ((adj_sources - last) ^ (side * (pulled_blocks // 2)))
    return jnp.where(adj_sources < last, adj_sources ^ (side * (target_blocks // 2)), pulled)


def layer(low, mask, features, history, adj_values, adj_sources, pull_list, pull_count, weight, bias):
    picked, dead, pieces = transfers(
        low, features, history, adj_sources, pull_list, pull_count, weight, mask > 0
    )
    mask_bits = lax.axis_size("dp").bit_length() - 1
    done = DIGIT_BITS
    if done < mask_bits:
        table = jnp.concatenate([array[start : start + rows] for array, start, rows in pieces])
        rows = features.shape[0]
        partner = table[rows : 2 * rows]
        while done < mask_bits:
            bits = min(DIGIT_BITS, mask_bits - done)
            moves = [
                functools.partial(lambda d, value: swap(value, "dp", d), digit << done)
                for digit in range(1, 1 << bits)
            ]
            partner = lax.switch((mask >> done) % (1 << bits), [lambda value: value] + moves, partner)
            done += bits
        parts = [table[:rows], partner, table[2 * rows :]]
        pieces = [(part, 0, part.shape[0]) for part in parts]
    return aggregate(picked, dead, adj_values, bias, pieces)


def per_device(
    features, history, adj_values, adj_sources, pull_list, pull_count, partner_mask, weight, bias
):
    mask = partner_mask[0]
    mask_bits = lax.axis_size("dp").bit_length() - 1
    digits = 1 << min(DIGIT_BITS, mask_bits)
    first = 1 if mask_bits <= DIGIT_BITS else 0
    return lax.switch(
        mask % digits - first,
        [functools.partial(layer, low) for low in range(first, digits)],
        mask,
        features,
        history,
        adj_values,
        adj_sources,
        pull_list[0],
        pull_count[0],
        weight,
        bias,
    )


def solution(mesh):
    in_specs = (
        P("dp", "mp"),
        P("dp", "mp"),
        P("dp", None, None, None),
        P("dp", None),
        P("dp", None, None),
        P("dp", None),
        P(),
        P("mp", None),
        P("mp"),
    )
    out_specs = P("dp", "mp")
    return jax.shard_map(
        per_device, mesh=mesh, in_specs=in_specs, out_specs=out_specs, check_vma=False
    )
```

```python
import functools
import math

import jax
import jax.numpy as jnp
from jax import lax
from jax.experimental import pallas as pl
from jax.experimental.pallas import tpu as pltpu
from jax.sharding import PartitionSpec as P

BLOCK = 128
FIRST = 9
ROWS = 512
UNROLL = 8
CHUNKS = 2
TILE = 1024
DIGIT_BITS = 3
VMEM = 32 * 1024 * 1024
SUM_VMEM = 56 * 1024 * 1024


def swap(value, axis, distance):
    pairs = [(source, source ^ distance) for source in range(lax.axis_size(axis))]
    return lax.ppermute(value, axis, pairs)


def swap_both(value, dp_distance, mp_distance):
    dp, mp = lax.axis_size("dp"), lax.axis_size("mp")
    pairs = [(i * mp + j, (i ^ dp_distance) * mp + (j ^ mp_distance)) for i in range(dp) for j in range(mp)]
    return lax.ppermute(value, ("dp", "mp"), pairs)


def after(value, *others):
    return lax.optimization_barrier((value, *others))[0]


def sealed(step, go, *values):
    shapes = jax.eval_shape(step, *values)
    empty = lambda *_: jax.tree.map(lambda leaf: jnp.zeros(leaf.shape, leaf.dtype), shapes)
    return lax.cond(go, step, empty, *values)


def side_of(halves, side):
    return lax.dynamic_index_in_dim(halves, (lax.axis_index("mp") % 2) ^ side, 0, keepdims=False)


def far(value):
    return [swap(value, "mp", d) for d in range(2, lax.axis_size("mp"), 2)]


def mix_kernel(count, side, mine, near, *refs):
    others, weights, (out, out_near) = refs[:-count - 2], refs[-count - 2 : -2], refs[-2:]
    width = out.shape[1]
    step = max(n for n in range(32, ROWS + 1, 32) if out.shape[0] % n == 0)

    def some(i, carry):
        at = pl.ds(pl.multiple_of(i * step, step), step)
        parts = [mine[0, at], near[at]]
        for other in others:
            parts += [other[0, at], other[1, at]] if len(other.shape) == 3 else [other[at]]
        total = jnp.dot(parts[0], weights[0][...], preferred_element_type=jnp.float32)
        for part, weight in zip(parts[1:], weights[1:]):
            total += jnp.dot(part, weight[...], preferred_element_type=jnp.float32)
        left, right = total[:, :width].astype(out.dtype), total[:, width:].astype(out.dtype)
        out[at] = jnp.where(side[0] == 0, left, right)
        out_near[at] = jnp.where(side[0] == 0, right, left)
        return carry

    lax.fori_loop(0, out.shape[0] // step, some, 0)


def tile_of(*counts):
    common = math.gcd(*counts)
    return max(n for n in range(BLOCK, TILE + 1, BLOCK) if common % n == 0)


def mix(halves, near, others, weights, start, end, others_from=0):
    rows, depth = end - start, near.shape[1]
    width = weights[0].shape[1] // 2
    tile = tile_of(rows, start, others_from)
    shift, skip = start // tile, (start - others_from) // tile
    pair = pl.BlockSpec((2, tile, depth), lambda i, _: (0, i + skip, 0))
    flat = pl.BlockSpec((tile, depth), lambda i, _: (i + skip, 0))
    grid_spec = pltpu.PrefetchScalarGridSpec(
        num_scalar_prefetch=1,
        grid=(rows // tile,),
        in_specs=[
            pl.BlockSpec((1, tile, depth), lambda i, side: (side[0], i + shift, 0)),
            pl.BlockSpec((tile, depth), lambda i, _: (i + shift, 0)),
        ]
        + [pair if other.ndim == 3 else flat for other in others]
        + [pl.BlockSpec(weight.shape, lambda i, _: (0, 0)) for weight in weights],
        out_specs=[pl.BlockSpec((tile, width), lambda i, _: (i, 0))] * 2,
    )
    return pl.pallas_call(
        functools.partial(mix_kernel, len(weights)),
        grid_spec=grid_spec,
        out_shape=[jax.ShapeDtypeStruct((rows, width), jnp.bfloat16)] * 2,
        compiler_params=pltpu.CompilerParams(vmem_limit_bytes=VMEM),
        cost_estimate=pl.CostEstimate(
            flops=2 * rows * depth * 2 * width * len(weights),
            bytes_accessed=2 * rows * (len(weights) * depth + 2 * width),
            transcendentals=0,
        ),
    )((lax.axis_index("mp") % 2).reshape(1), halves, near, *others, *weights)


def agg_kernel(where, target_blocks, adj_sources, pull_count, side, adj, bias, *rest):
    *sources, out, table, sems = rest
    step = pl.program_id(0)
    group, tiles = adj.shape[0], adj.shape[1]
    last = 2 * target_blocks
    pulled_blocks = table.shape[0] // BLOCK - last
    slots = pulled_blocks // pull_count.shape[0]

    def place(block):
        half = jnp.where(block < last, target_blocks, pulled_blocks) // 2
        return jnp.where(side[0] == 0, block, jnp.where(block < last, block ^ half, ((block - last) ^ half) + last))

    @pl.when(step == 0)
    def _():
        copies = []
        for i, (which, start, rows, row) in enumerate(where):
            source = sources[which].at[pl.ds(start, rows)]
            copies.append(pltpu.make_async_copy(source, table.at[pl.ds(row, rows)], sems.at[i]))
        for copy in copies:
            copy.start()
        for copy in copies:
            copy.wait()

        def clear(slot, carry):
            @pl.when(slot % slots >= pull_count[slot // slots])
            def _():
                row = pl.multiple_of(place(2 * target_blocks + slot) * BLOCK, BLOCK)
                table[pl.ds(row, BLOCK), :] = jnp.zeros((BLOCK, table.shape[1]), table.dtype)

            return carry

        lax.fori_loop(0, pulled_blocks, clear, 0)

    def some(i, _):
        for u in range(UNROLL):
            t = i * UNROLL + u
            lhs = jnp.concatenate([adj[t, k] for k in range(tiles)], axis=1)
            picks = []
            for k in range(tiles):
                row = pl.multiple_of(place(adj_sources[(step * group + t) * tiles + k]) * BLOCK, BLOCK)
                picks.append(table[pl.ds(row, BLOCK), :])
            total = jnp.dot(lhs, jnp.concatenate(picks, axis=0), preferred_element_type=jnp.float32)
            row = pl.multiple_of(t * BLOCK, BLOCK)
            out[pl.ds(row, BLOCK), :] = jnp.maximum(total + bias[...], 0.0).astype(out.dtype)
        return _

    lax.fori_loop(0, group // UNROLL, some, 0)


def aggregate(adj_sources, pull_count, adj_values, bias, pieces):
    target_blocks, tiles = adj_values.shape[:2]
    width = bias.shape[0]
    group = math.gcd(target_blocks, 8)
    arrays, where, total_rows = [], [], 0
    for array, start, rows in pieces:
        known = [i for i, a in enumerate(arrays) if a is array]
        if not known:
            arrays.append(array)
        where.append((known[0] if known else len(arrays) - 1, start, rows, total_rows))
        total_rows += rows
    grid_spec = pltpu.PrefetchScalarGridSpec(
        num_scalar_prefetch=3,
        grid=(target_blocks // group,),
        in_specs=[
            pl.BlockSpec((group, tiles, BLOCK, BLOCK), lambda i, *_: (i, 0, 0, 0)),
            pl.BlockSpec((1, width), lambda i, *_: (0, 0)),
        ]
        + [pl.BlockSpec(memory_space=pl.ANY)] * len(arrays),
        out_specs=pl.BlockSpec((group * BLOCK, width), lambda i, *_: (i, 0)),
        scratch_shapes=[
            pltpu.VMEM((total_rows, width), jnp.bfloat16),
            pltpu.SemaphoreType.DMA((len(where),)),
        ],
    )
    return pl.pallas_call(
        functools.partial(agg_kernel, where, target_blocks),
        grid_spec=grid_spec,
        out_shape=pltpu.HBM((target_blocks * BLOCK, width), jnp.bfloat16),
        compiler_params=pltpu.CompilerParams(vmem_limit_bytes=SUM_VMEM),
        cost_estimate=pl.CostEstimate(
            flops=2 * target_blocks * tiles * BLOCK * BLOCK * width,
            bytes_accessed=2 * (target_blocks * tiles * BLOCK * BLOCK + total_rows * width),
            transcendentals=0,
        ),
    )(adj_sources, pull_count, (lax.axis_index("mp") % 2).reshape(1), adj_values, bias.reshape(1, -1), *arrays)


def far_weight(weight):
    mp_count = lax.axis_size("mp")
    chip = lax.axis_index("mp") // 2
    both = 2 * weight.shape[1] // mp_count
    pairs = []
    for d in range(mp_count // 2):
        pair = lax.dynamic_slice_in_dim(weight, (chip ^ d) * both, both, axis=1)
        pairs.append(swap(pair, "mp", 2 * d) if d else pair)
    return pairs


def all_weight(*pairs):
    return [part for pair in pairs for part in (pair, swap(pair, "mp", 1))]


def transfers(low, features, history, adj_sources, pull_list, weight, go):
    depth = features.shape[1]
    halves = features.reshape(2, -1, depth)
    rows = halves.shape[1]
    cut = rows * FIRST // 16
    send = [(0, cut), (cut, rows)]

    wanted = lax.all_to_all(pull_list, "dp", split_axis=0, concat_axis=0, tiled=True)
    weights = far_weight(weight)
    mine = side_of(halves, 0)
    near = swap(side_of(halves, 1), "mp", 1)
    sent = after(mine, *weights)
    crossed = [far(jnp.stack([sent[start:end], near[start:end]])) for start, end in send]

    def spread_weight(adj_sources, *pairs):
        return adj_sources.reshape(-1), all_weight(*pairs)

    adj_sources, columns = sealed(spread_weight, go, adj_sources, after(weights[0], near), *weights[1:])
    picked = history.reshape(-1, BLOCK, depth)[wanted]
    pulled = lax.all_to_all(picked, "dp", split_axis=0, concat_axis=0, tiled=True)

    def to_partner(here, beside):
        return (swap(here, "dp", low) if low else here), swap_both(beside, low, 1)

    def settle(columns, foreign, beside):
        near = swap(side_of(foreign, 1), "mp", 1)
        others = far(jnp.stack([side_of(foreign, 0), near]))
        here, foreign_beside = mix(foreign, near, others, columns, 0, near.shape[0])
        beside = swap(after(beside, *others), "mp", 1)
        return here, [beside, swap(after(foreign_beside, beside), "mp", 1)]

    first, rest = crossed
    own, beside = mix(halves, near, first, columns, 0, cut)
    moved = to_partner(own, beside)
    own_near = swap(beside, "mp", 1)
    rest[0] = after(rest[0], own, own_near)
    own_rest, beside = mix(halves, near, rest, columns, cut, rows, cut)
    moved_rest = to_partner(own_rest, beside)
    foreign = after(pulled, own_rest).reshape(2, -1, depth)
    foreign, swapped = sealed(settle, go, columns, foreign, beside)
    table = [own, own_rest, own_near, swapped[0], moved[0], moved_rest[0], moved[1], moved_rest[1]]
    return adj_sources, [*table, foreign, swapped[-1]]


def per_device(
    features, history, adj_values, adj_sources, pull_list, pull_count, partner_mask, weight, bias
):
    mask = partner_mask[0]
    mask_bits = lax.axis_size("dp").bit_length() - 1
    done = min(DIGIT_BITS, mask_bits)
    first = 1 if mask_bits <= DIGIT_BITS else 0
    adj_sources, tables = lax.switch(
        mask % (1 << done) - first,
        [functools.partial(transfers, low) for low in range(first, 1 << done)],
        features,
        history,
        adj_sources,
        pull_list[0],
        weight,
        mask > 0,
    )
    own, partner, pulled = tables[:4], tables[4:8], tables[8:]
    while done < mask_bits:
        bits = min(DIGIT_BITS, mask_bits - done)
        moves = [
            functools.partial(lambda d, *values: [swap(value, "dp", d) for value in values], digit << done)
            for digit in range(1, 1 << bits)
        ]
        partner = lax.switch((mask >> done) % (1 << bits), [lambda *values: list(values)] + moves, *partner)
        done += bits
    pieces = [(value, 0, value.shape[0]) for value in [*own, *partner, *pulled]]
    return aggregate(adj_sources, pull_count[0], adj_values, bias, pieces)


def solution(mesh):
    in_specs = (
        P("dp", "mp"),
        P("dp", "mp"),
        P("dp", None, None, None),
        P("dp", None),
        P("dp", None, None),
        P("dp", None),
        P(),
        P("mp", None),
        P("mp"),
    )
    out_specs = P("dp", "mp")
    return jax.shard_map(
        per_device, mesh=mesh, in_specs=in_specs, out_specs=out_specs, check_vma=False
    )
```

```python
import functools
import math

import jax
import jax.numpy as jnp
from jax import lax
from jax.experimental import pallas as pl
from jax.experimental.pallas import tpu as pltpu
from jax.sharding import PartitionSpec as P

BLOCK = 128
FIRST = 8
ROWS = 512
UNROLL = 16
CHUNKS = 2
TILE = 1024
DIGIT_BITS = 3
VMEM = 32 * 1024 * 1024
SUM_VMEM = 56 * 1024 * 1024


def swap(value, axis, distance):
    pairs = [(source, source ^ distance) for source in range(lax.axis_size(axis))]
    return lax.ppermute(value, axis, pairs)


def swap_both(value, dp_distance, mp_distance):
    dp, mp = lax.axis_size("dp"), lax.axis_size("mp")
    pairs = [(i * mp + j, (i ^ dp_distance) * mp + (j ^ mp_distance)) for i in range(dp) for j in range(mp)]
    return lax.ppermute(value, ("dp", "mp"), pairs)


def after(value, *others):
    return lax.optimization_barrier((value, *others))[0]


def sealed(step, go, *values):
    shapes = jax.eval_shape(step, *values)
    empty = lambda *_: jax.tree.map(lambda leaf: jnp.zeros(leaf.shape, leaf.dtype), shapes)
    return lax.cond(go, step, empty, *values)


def side_of(halves, side):
    return lax.dynamic_index_in_dim(halves, (lax.axis_index("mp") % 2) ^ side, 0, keepdims=False)


def far(value):
    return [swap(value, "mp", d) for d in range(2, lax.axis_size("mp"), 2)]


def mix_kernel(count, side, mine, near, *refs):
    others, weights, (out, out_near) = refs[:-count - 2], refs[-count - 2 : -2], refs[-2:]
    width = out.shape[1]
    step = max(n for n in range(32, ROWS + 1, 32) if out.shape[0] % n == 0)

    def some(i, carry):
        at = pl.ds(pl.multiple_of(i * step, step), step)
        parts = [mine[0, at], near[at]]
        for other in others:
            parts += [other[0, at], other[1, at]] if len(other.shape) == 3 else [other[at]]
        total = jnp.dot(parts[0], weights[0][...], preferred_element_type=jnp.float32)
        for part, weight in zip(parts[1:], weights[1:]):
            total += jnp.dot(part, weight[...], preferred_element_type=jnp.float32)
        left, right = total[:, :width].astype(out.dtype), total[:, width:].astype(out.dtype)
        out[at] = jnp.where(side[0] == 0, left, right)
        out_near[at] = jnp.where(side[0] == 0, right, left)
        return carry

    lax.fori_loop(0, out.shape[0] // step, some, 0)


def tile_of(*counts):
    common = math.gcd(*counts)
    return max(n for n in range(BLOCK, TILE + 1, BLOCK) if common % n == 0)


def mix(halves, near, others, weights, start, end, others_from=0):
    rows, depth = end - start, near.shape[1]
    width = weights[0].shape[1] // 2
    tile = tile_of(rows, start, others_from)
    shift, skip = start // tile, (start - others_from) // tile
    pair = pl.BlockSpec((2, tile, depth), lambda i, _: (0, i + skip, 0))
    flat = pl.BlockSpec((tile, depth), lambda i, _: (i + skip, 0))
    grid_spec = pltpu.PrefetchScalarGridSpec(
        num_scalar_prefetch=1,
        grid=(rows // tile,),
        in_specs=[
            pl.BlockSpec((1, tile, depth), lambda i, side: (side[0], i + shift, 0)),
            pl.BlockSpec((tile, depth), lambda i, _: (i + shift, 0)),
        ]
        + [pair if other.ndim == 3 else flat for other in others]
        + [pl.BlockSpec(weight.shape, lambda i, _: (0, 0)) for weight in weights],
        out_specs=[pl.BlockSpec((tile, width), lambda i, _: (i, 0))] * 2,
    )
    return pl.pallas_call(
        functools.partial(mix_kernel, len(weights)),
        grid_spec=grid_spec,
        out_shape=[jax.ShapeDtypeStruct((rows, width), jnp.bfloat16)] * 2,
        compiler_params=pltpu.CompilerParams(vmem_limit_bytes=VMEM),
        cost_estimate=pl.CostEstimate(
            flops=2 * rows * depth * 2 * width * len(weights),
            bytes_accessed=2 * rows * (len(weights) * depth + 2 * width),
            transcendentals=0,
        ),
    )((lax.axis_index("mp") % 2).reshape(1), halves, near, *others, *weights)


def agg_kernel(where, source_rows, pull_count, side, bias, adj, *rest):
    *sources, out, table, tiles_of, rows_of, table_sems, adj_sems, out_sems = rest
    target_blocks, tiles = adj.shape[:2]
    last = 2 * target_blocks
    pulled_blocks = table.shape[0] // BLOCK - last
    slots = pulled_blocks // pull_count.shape[0]
    groups = target_blocks // UNROLL

    def tiles_in(group):
        here = pl.ds(group * UNROLL, UNROLL)
        return pltpu.make_async_copy(adj.at[here], tiles_of.at[here], adj_sems.at[group])

    def rows_out(group):
        here = pl.ds(pl.multiple_of(group * UNROLL * BLOCK, BLOCK), UNROLL * BLOCK)
        return pltpu.make_async_copy(rows_of.at[here], out.at[here], out_sems.at[group])

    copies = []
    for i, (which, rows, row) in enumerate(where):
        copies.append(pltpu.make_async_copy(sources[which], table.at[pl.ds(row, rows)], table_sems.at[i]))
        copies[-1].start()
    for group in range(groups):
        tiles_in(group).start()
    for copy in copies:
        copy.wait()

    def clear(slot, carry):
        @pl.when(slot % slots >= pull_count[slot // slots])
        def _():
            row = pl.multiple_of((last + (slot ^ (side[0] * (pulled_blocks // 2)))) * BLOCK, BLOCK)
            table[pl.ds(row, BLOCK), :] = jnp.zeros((BLOCK, table.shape[1]), table.dtype)

        return carry

    lax.fori_loop(0, pulled_blocks, clear, 0)

    def some(group, carry):
        tiles_in(group).wait()
        for u in range(UNROLL):
            t = group * UNROLL + u
            lhs = jnp.concatenate([tiles_of[t, k] for k in range(tiles)], axis=1)
            picks = []
            for k in range(tiles):
                row = pl.multiple_of(source_rows[t * tiles + k], BLOCK)
                picks.append(table[pl.ds(row, BLOCK), :])
            total = jnp.dot(lhs, jnp.concatenate(picks, axis=0), preferred_element_type=jnp.float32)
            row = pl.multiple_of(t * BLOCK, BLOCK)
            rows_of[pl.ds(row, BLOCK), :] = jnp.maximum(total + bias[...], 0.0).astype(rows_of.dtype)
        rows_out(group).start()
        return carry

    lax.fori_loop(0, groups, some, 0)
    for group in range(groups):
        rows_out(group).wait()


def aggregate(source_rows, pull_count, adj_values, bias, tables):
    target_blocks, tiles = adj_values.shape[:2]
    width = bias.shape[0]
    where, total_rows = [], 0
    for i, array in enumerate(tables):
        where.append((i, array.shape[0], total_rows))
        total_rows += array.shape[0]
    groups = target_blocks // UNROLL
    grid_spec = pltpu.PrefetchScalarGridSpec(
        num_scalar_prefetch=3,
        grid=(1,),
        in_specs=[pl.BlockSpec((1, width), lambda i, *_: (0, 0))]
        + [pl.BlockSpec(memory_space=pl.ANY)] * (1 + len(tables)),
        out_specs=pl.BlockSpec(memory_space=pl.ANY),
        scratch_shapes=[
            pltpu.VMEM((total_rows, width), jnp.bfloat16),
            pltpu.VMEM(adj_values.shape, jnp.bfloat16),
            pltpu.VMEM((target_blocks * BLOCK, width), jnp.bfloat16),
            pltpu.SemaphoreType.DMA((len(where),)),
            pltpu.SemaphoreType.DMA((groups,)),
            pltpu.SemaphoreType.DMA((groups,)),
        ],
    )
    return pl.pallas_call(
        functools.partial(agg_kernel, where),
        grid_spec=grid_spec,
        out_shape=jax.ShapeDtypeStruct((target_blocks * BLOCK, width), jnp.bfloat16),
        compiler_params=pltpu.CompilerParams(vmem_limit_bytes=SUM_VMEM),
        cost_estimate=pl.CostEstimate(
            flops=2 * target_blocks * tiles * BLOCK * BLOCK * width,
            bytes_accessed=2 * (target_blocks * tiles * BLOCK * BLOCK + total_rows * width),
            transcendentals=0,
        ),
    )(source_rows, pull_count, (lax.axis_index("mp") % 2).reshape(1), bias.reshape(1, -1), adj_values, *tables)


def far_weight(weight):
    mp_count = lax.axis_size("mp")
    chip = lax.axis_index("mp") // 2
    both = 2 * weight.shape[1] // mp_count
    pairs = []
    for d in range(mp_count // 2):
        pair = lax.dynamic_slice_in_dim(weight, (chip ^ d) * both, both, axis=1)
        pairs.append(swap(pair, "mp", 2 * d) if d else pair)
    return pairs


def all_weight(*pairs):
    return [part for pair in pairs for part in (pair, swap(pair, "mp", 1))]


def transfers(low, features, history, adj_sources, pull_list, weight, go):
    depth = features.shape[1]
    halves = features.reshape(2, -1, depth)
    rows = halves.shape[1]
    cut = rows * FIRST // 16
    send = [(0, cut), (cut, rows)]

    weights = far_weight(weight)
    wanted = lax.all_to_all(after(pull_list, *weights), "dp", split_axis=0, concat_axis=0, tiled=True)
    mine = side_of(halves, 0)
    near = swap(side_of(halves, 1), "mp", 1)
    sent = mine
    crossed = [far(jnp.stack([sent[start:end], near[start:end]])) for start, end in send]

    def spread_weight(adj_sources, *pairs):
        blocks = adj_sources.reshape(-1)
        side = lax.axis_index("mp") % 2
        last = 2 * features.shape[0] // BLOCK
        pulled_blocks = pull_list.size
        half = jnp.where(blocks < last, last // 2, pulled_blocks) // 2
        moved = jnp.where(blocks < last, blocks ^ half, ((blocks - last) ^ half) + last)
        return jnp.where(side == 0, blocks, moved) * BLOCK, all_weight(*pairs)

    source_rows, columns = sealed(spread_weight, go, adj_sources, after(weights[0], near), *weights[1:])
    picked = history.reshape(-1, BLOCK, depth)[wanted]
    pulled = lax.all_to_all(picked, "dp", split_axis=0, concat_axis=0, tiled=True)

    def to_partner(here, beside):
        return (swap(here, "dp", low) if low else here), swap_both(beside, low, 1)

    def settle(columns, foreign, beside):
        near = swap(side_of(foreign, 1), "mp", 1)
        others = far(jnp.stack([side_of(foreign, 0), near]))
        here, foreign_beside = mix(foreign, near, others, columns, 0, near.shape[0])
        beside = swap(after(beside, *others), "mp", 1)
        return here, [beside, swap(after(foreign_beside, beside), "mp", 1)]

    first, rest = crossed
    own, beside = mix(halves, near, first, columns, 0, cut)
    moved = to_partner(own, beside)
    own_near = swap(beside, "mp", 1)
    rest[0] = after(rest[0], own, own_near)
    own_rest, beside = mix(halves, near, rest, columns, cut, rows, cut)
    moved_rest = to_partner(own_rest, beside)
    foreign = after(pulled, own_rest).reshape(2, -1, depth)
    foreign, swapped = sealed(settle, go, columns, foreign, beside)
    table = [own, own_rest, own_near, swapped[0], moved[0], moved_rest[0], moved[1], moved_rest[1]]
    return source_rows, [*table, foreign, swapped[-1]]


def per_device(
    features, history, adj_values, adj_sources, pull_list, pull_count, partner_mask, weight, bias
):
    mask = partner_mask[0]
    mask_bits = lax.axis_size("dp").bit_length() - 1
    done = min(DIGIT_BITS, mask_bits)
    first = 1 if mask_bits <= DIGIT_BITS else 0
    source_rows, tables = lax.switch(
        mask % (1 << done) - first,
        [functools.partial(transfers, low) for low in range(first, 1 << done)],
        features,
        history,
        adj_sources,
        pull_list[0],
        weight,
        mask > 0,
    )
    own, partner, pulled = tables[:4], tables[4:8], tables[8:]
    while done < mask_bits:
        bits = min(DIGIT_BITS, mask_bits - done)
        moves = [
            functools.partial(lambda d, *values: [swap(value, "dp", d) for value in values], digit << done)
            for digit in range(1, 1 << bits)
        ]
        partner = lax.switch((mask >> done) % (1 << bits), [lambda *values: list(values)] + moves, *partner)
        done += bits
    return aggregate(source_rows, pull_count[0], adj_values, bias, [*own, *partner, *pulled])


def solution(mesh):
    in_specs = (
        P("dp", "mp"),
        P("dp", "mp"),
        P("dp", None, None, None),
        P("dp", None),
        P("dp", None, None),
        P("dp", None),
        P(),
        P("mp", None),
        P("mp"),
    )
    out_specs = P("dp", "mp")
    return jax.shard_map(
        per_device, mesh=mesh, in_specs=in_specs, out_specs=out_specs, check_vma=False
    )
```

```python
import functools
import math

import jax
import jax.numpy as jnp
from jax import lax
from jax.experimental import pallas as pl
from jax.experimental.pallas import tpu as pltpu
from jax.sharding import PartitionSpec as P

BLOCK = 128
FIRST = 8
ROWS = 512
UNROLL = 16
CHUNKS = 2
TILE = 1024
DIGIT_BITS = 3
VMEM = 32 * 1024 * 1024
SUM_VMEM = 56 * 1024 * 1024


def swap(value, axis, distance):
    pairs = [(source, source ^ distance) for source in range(lax.axis_size(axis))]
    return lax.ppermute(value, axis, pairs)


def swap_both(value, dp_distance, mp_distance):
    dp, mp = lax.axis_size("dp"), lax.axis_size("mp")
    pairs = [(i * mp + j, (i ^ dp_distance) * mp + (j ^ mp_distance)) for i in range(dp) for j in range(mp)]
    return lax.ppermute(value, ("dp", "mp"), pairs)


def after(value, *others):
    return lax.optimization_barrier((value, *others))[0]


def sealed(step, go, *values):
    shapes = jax.eval_shape(step, *values)
    empty = lambda *_: jax.tree.map(lambda leaf: jnp.zeros(leaf.shape, leaf.dtype), shapes)
    return lax.cond(go, step, empty, *values)


def side_of(halves, side):
    return lax.dynamic_index_in_dim(halves, (lax.axis_index("mp") % 2) ^ side, 0, keepdims=False)


def far(value):
    return [swap(value, "mp", d) for d in range(2, lax.axis_size("mp"), 2)]


def mix_kernel(count, side, mine, near, *refs):
    others, weights, (out, out_near) = refs[:-count - 2], refs[-count - 2 : -2], refs[-2:]
    width = out.shape[1]
    step = max(n for n in range(32, ROWS + 1, 32) if out.shape[0] % n == 0)

    def some(i, carry):
        at = pl.ds(pl.multiple_of(i * step, step), step)
        parts = [mine[0, at], near[at]]
        for other in others:
            parts += [other[0, at], other[1, at]] if len(other.shape) == 3 else [other[at]]
        total = jnp.dot(parts[0], weights[0][...], preferred_element_type=jnp.float32)
        for part, weight in zip(parts[1:], weights[1:]):
            total += jnp.dot(part, weight[...], preferred_element_type=jnp.float32)
        left, right = total[:, :width].astype(out.dtype), total[:, width:].astype(out.dtype)
        out[at] = jnp.where(side[0] == 0, left, right)
        out_near[at] = jnp.where(side[0] == 0, right, left)
        return carry

    lax.fori_loop(0, out.shape[0] // step, some, 0)


def tile_of(*counts):
    common = math.gcd(*counts)
    return max(n for n in range(BLOCK, TILE + 1, BLOCK) if common % n == 0)


def mix(halves, near, others, weights, start, end, others_from=0):
    rows, depth = end - start, near.shape[1]
    width = weights[0].shape[1] // 2
    tile = tile_of(rows, start, others_from)
    shift, skip = start // tile, (start - others_from) // tile
    pair = pl.BlockSpec((2, tile, depth), lambda i, _: (0, i + skip, 0))
    flat = pl.BlockSpec((tile, depth), lambda i, _: (i + skip, 0))
    grid_spec = pltpu.PrefetchScalarGridSpec(
        num_scalar_prefetch=1,
        grid=(rows // tile,),
        in_specs=[
            pl.BlockSpec((1, tile, depth), lambda i, side: (side[0], i + shift, 0)),
            pl.BlockSpec((tile, depth), lambda i, _: (i + shift, 0)),
        ]
        + [pair if other.ndim == 3 else flat for other in others]
        + [pl.BlockSpec(weight.shape, lambda i, _: (0, 0)) for weight in weights],
        out_specs=[pl.BlockSpec((tile, width), lambda i, _: (i, 0))] * 2,
    )
    return pl.pallas_call(
        functools.partial(mix_kernel, len(weights)),
        grid_spec=grid_spec,
        out_shape=[jax.ShapeDtypeStruct((rows, width), jnp.bfloat16)] * 2,
        compiler_params=pltpu.CompilerParams(vmem_limit_bytes=VMEM),
        cost_estimate=pl.CostEstimate(
            flops=2 * rows * depth * 2 * width * len(weights),
            bytes_accessed=2 * rows * (len(weights) * depth + 2 * width),
            transcendentals=0,
        ),
    )((lax.axis_index("mp") % 2).reshape(1), halves, near, *others, *weights)


def agg_kernel(where, source_rows, pull_count, side, bias, adj, *rest):
    *sources, out, table, tiles_of, rows_of, table_sems, adj_sems, out_sems = rest
    target_blocks, tiles = adj.shape[:2]
    last = 2 * target_blocks
    pulled_blocks = table.shape[0] // BLOCK - last
    slots = pulled_blocks // pull_count.shape[0]
    groups = target_blocks // UNROLL

    def tiles_in(group):
        here = pl.ds(group * UNROLL, UNROLL)
        return pltpu.make_async_copy(adj.at[here], tiles_of.at[here], adj_sems.at[group])

    def rows_out(group):
        here = pl.ds(pl.multiple_of(group * UNROLL * BLOCK, BLOCK), UNROLL * BLOCK)
        return pltpu.make_async_copy(rows_of.at[here], out.at[here], out_sems.at[group])

    copies = []
    for i, (which, rows, row) in enumerate(where):
        copies.append(pltpu.make_async_copy(sources[which], table.at[pl.ds(row, rows)], table_sems.at[i]))
        copies[-1].start()
    for group in range(groups):
        tiles_in(group).start()
    for copy in copies:
        copy.wait()

    def clear(slot, carry):
        @pl.when(slot % slots >= pull_count[slot // slots])
        def _():
            row = pl.multiple_of((last + (slot ^ (side[0] * (pulled_blocks // 2)))) * BLOCK, BLOCK)
            table[pl.ds(row, BLOCK), :] = jnp.zeros((BLOCK, table.shape[1]), table.dtype)

        return carry

    lax.fori_loop(0, pulled_blocks, clear, 0)

    def some(group, carry):
        tiles_in(group).wait()
        for u in range(UNROLL):
            t = group * UNROLL + u
            lhs = jnp.concatenate([tiles_of[t, k] for k in range(tiles)], axis=1)
            picks = []
            for k in range(tiles):
                row = pl.multiple_of(source_rows[t * tiles + k], BLOCK)
                picks.append(table[pl.ds(row, BLOCK), :])
            total = jnp.dot(lhs, jnp.concatenate(picks, axis=0), preferred_element_type=jnp.float32)
            row = pl.multiple_of(t * BLOCK, BLOCK)
            rows_of[pl.ds(row, BLOCK), :] = jnp.maximum(total + bias[...], 0.0).astype(rows_of.dtype)
        rows_out(group).start()
        return carry

    lax.fori_loop(0, groups, some, 0)
    for group in range(groups):
        rows_out(group).wait()


def aggregate(source_rows, pull_count, adj_values, bias, tables):
    target_blocks, tiles = adj_values.shape[:2]
    width = bias.shape[0]
    where, total_rows = [], 0
    for i, array in enumerate(tables):
        where.append((i, array.shape[0], total_rows))
        total_rows += array.shape[0]
    groups = target_blocks // UNROLL
    grid_spec = pltpu.PrefetchScalarGridSpec(
        num_scalar_prefetch=3,
        grid=(1,),
        in_specs=[pl.BlockSpec((1, width), lambda i, *_: (0, 0))]
        + [pl.BlockSpec(memory_space=pl.ANY)] * (1 + len(tables)),
        out_specs=pl.BlockSpec(memory_space=pl.ANY),
        scratch_shapes=[
            pltpu.VMEM((total_rows, width), jnp.bfloat16),
            pltpu.VMEM(adj_values.shape, jnp.bfloat16),
            pltpu.VMEM((target_blocks * BLOCK, width), jnp.bfloat16),
            pltpu.SemaphoreType.DMA((len(where),)),
            pltpu.SemaphoreType.DMA((groups,)),
            pltpu.SemaphoreType.DMA((groups,)),
        ],
    )
    return pl.pallas_call(
        functools.partial(agg_kernel, where),
        grid_spec=grid_spec,
        out_shape=jax.ShapeDtypeStruct((target_blocks * BLOCK, width), jnp.bfloat16),
        compiler_params=pltpu.CompilerParams(vmem_limit_bytes=SUM_VMEM),
        cost_estimate=pl.CostEstimate(
            flops=2 * target_blocks * tiles * BLOCK * BLOCK * width,
            bytes_accessed=2 * (target_blocks * tiles * BLOCK * BLOCK + total_rows * width),
            transcendentals=0,
        ),
    )(source_rows, pull_count, (lax.axis_index("mp") % 2).reshape(1), bias.reshape(1, -1), adj_values, *tables)


def far_weight(weight):
    mp_count = lax.axis_size("mp")
    chip = lax.axis_index("mp") // 2
    both = 2 * weight.shape[1] // mp_count
    pairs = []
    for d in range(mp_count // 2):
        pair = lax.dynamic_slice_in_dim(weight, (chip ^ d) * both, both, axis=1)
        pairs.append(swap(pair, "mp", 2 * d) if d else pair)
    return pairs


def all_weight(*pairs):
    return [part for pair in pairs for part in (pair, swap(pair, "mp", 1))]


def transfers(low, features, history, adj_sources, pull_list, weight, go):
    depth = features.shape[1]
    halves = features.reshape(2, -1, depth)
    rows = halves.shape[1]
    cut = rows * FIRST // 16
    send = [(0, cut), (cut, rows)]

    weights = far_weight(weight)
    mine = side_of(halves, 0)
    near = swap(side_of(halves, 1), "mp", 1)
    wanted = lax.all_to_all(after(pull_list, near), "dp", split_axis=0, concat_axis=0, tiled=True)
    sent = mine
    crossed = [far(jnp.stack([sent[start:end], near[start:end]])) for start, end in send]

    def spread_weight(adj_sources, *pairs):
        blocks = adj_sources.reshape(-1)
        side = lax.axis_index("mp") % 2
        last = 2 * features.shape[0] // BLOCK
        pulled_blocks = pull_list.size
        half = jnp.where(blocks < last, last // 2, pulled_blocks) // 2
        moved = jnp.where(blocks < last, blocks ^ half, ((blocks - last) ^ half) + last)
        return jnp.where(side == 0, blocks, moved) * BLOCK, all_weight(*pairs)

    source_rows, columns = sealed(spread_weight, go, adj_sources, after(weights[0], near), *weights[1:])
    picked = history.reshape(-1, BLOCK, depth)[after(wanted, *weights)]
    pulled = lax.all_to_all(picked, "dp", split_axis=0, concat_axis=0, tiled=True)

    def to_partner(here, beside):
        return (swap(here, "dp", low) if low else here), swap_both(beside, low, 1)

    def settle(columns, foreign, beside):
        near = swap(side_of(foreign, 1), "mp", 1)
        others = far(jnp.stack([side_of(foreign, 0), near]))
        here, foreign_beside = mix(foreign, near, others, columns, 0, near.shape[0])
        beside = swap(after(beside, *others), "mp", 1)
        return here, [beside, swap(after(foreign_beside, beside), "mp", 1)]

    first, rest = crossed
    own, beside = mix(halves, near, first, columns, 0, cut)
    moved = to_partner(own, beside)
    own_near = swap(beside, "mp", 1)
    rest[0] = after(rest[0], own, own_near)
    own_rest, beside = mix(halves, near, rest, columns, cut, rows, cut)
    moved_rest = to_partner(own_rest, beside)
    foreign = after(pulled, own_rest).reshape(2, -1, depth)
    foreign, swapped = sealed(settle, go, columns, foreign, beside)
    table = [own, own_rest, own_near, swapped[0], moved[0], moved_rest[0], moved[1], moved_rest[1]]
    return source_rows, [*table, foreign, swapped[-1]]


def per_device(
    features, history, adj_values, adj_sources, pull_list, pull_count, partner_mask, weight, bias
):
    mask = partner_mask[0]
    mask_bits = lax.axis_size("dp").bit_length() - 1
    done = min(DIGIT_BITS, mask_bits)
    first = 1 if mask_bits <= DIGIT_BITS else 0
    source_rows, tables = lax.switch(
        mask % (1 << done) - first,
        [functools.partial(transfers, low) for low in range(first, 1 << done)],
        features,
        history,
        adj_sources,
        pull_list[0],
        weight,
        mask > 0,
    )
    own, partner, pulled = tables[:4], tables[4:8], tables[8:]
    while done < mask_bits:
        bits = min(DIGIT_BITS, mask_bits - done)
        moves = [
            functools.partial(lambda d, *values: [swap(value, "dp", d) for value in values], digit << done)
            for digit in range(1, 1 << bits)
        ]
        partner = lax.switch((mask >> done) % (1 << bits), [lambda *values: list(values)] + moves, *partner)
        done += bits
    return aggregate(source_rows, pull_count[0], adj_values, bias, [*own, *partner, *pulled])


def solution(mesh):
    in_specs = (
        P("dp", "mp"),
        P("dp", "mp"),
        P("dp", None, None, None),
        P("dp", None),
        P("dp", None, None),
        P("dp", None),
        P(),
        P("mp", None),
        P("mp"),
    )
    out_specs = P("dp", "mp")
    return jax.shard_map(
        per_device, mesh=mesh, in_specs=in_specs, out_specs=out_specs, check_vma=False
    )
```

```python
import functools
import math

import jax
import jax.numpy as jnp
from jax import lax
from jax.experimental import pallas as pl
from jax.experimental.pallas import tpu as pltpu
from jax.sharding import PartitionSpec as P

BLOCK = 128
FIRST = 8
ROWS = 512
UNROLL = 16
CHUNKS = 2
TILE = 1024
DIGIT_BITS = 3
VMEM = 32 * 1024 * 1024
SUM_VMEM = 56 * 1024 * 1024


def swap(value, axis, distance):
    pairs = [(source, source ^ distance) for source in range(lax.axis_size(axis))]
    return lax.ppermute(value, axis, pairs)


def swap_both(value, dp_distance, mp_distance):
    dp, mp = lax.axis_size("dp"), lax.axis_size("mp")
    pairs = [(i * mp + j, (i ^ dp_distance) * mp + (j ^ mp_distance)) for i in range(dp) for j in range(mp)]
    return lax.ppermute(value, ("dp", "mp"), pairs)


def after(value, *others):
    return lax.optimization_barrier((value, *others))[0]


def sealed(step, go, *values):
    shapes = jax.eval_shape(step, *values)
    empty = lambda *_: jax.tree.map(lambda leaf: jnp.zeros(leaf.shape, leaf.dtype), shapes)
    return lax.cond(go, step, empty, *values)


def side_of(halves, side):
    return lax.dynamic_index_in_dim(halves, (lax.axis_index("mp") % 2) ^ side, 0, keepdims=False)


def far(value):
    return [swap(value, "mp", d) for d in range(2, lax.axis_size("mp"), 2)]


def mix_kernel(count, side, mine, near, *refs):
    others, weights, (out, out_near) = refs[:-count - 2], refs[-count - 2 : -2], refs[-2:]
    width = out.shape[1]
    step = max(n for n in range(32, ROWS + 1, 32) if out.shape[0] % n == 0)

    def some(i, carry):
        at = pl.ds(pl.multiple_of(i * step, step), step)
        parts = [mine[0, at], near[at]]
        for other in others:
            parts += [other[0, at], other[1, at]] if len(other.shape) == 3 else [other[at]]
        total = jnp.dot(parts[0], weights[0][...], preferred_element_type=jnp.float32)
        for part, weight in zip(parts[1:], weights[1:]):
            total += jnp.dot(part, weight[...], preferred_element_type=jnp.float32)
        left, right = total[:, :width].astype(out.dtype), total[:, width:].astype(out.dtype)
        out[at] = jnp.where(side[0] == 0, left, right)
        out_near[at] = jnp.where(side[0] == 0, right, left)
        return carry

    lax.fori_loop(0, out.shape[0] // step, some, 0)


def tile_of(*counts):
    common = math.gcd(*counts)
    return max(n for n in range(BLOCK, TILE + 1, BLOCK) if common % n == 0)


def mix(halves, near, others, weights, start, end, others_from=0):
    rows, depth = end - start, near.shape[1]
    width = weights[0].shape[1] // 2
    tile = tile_of(rows, start, others_from)
    shift, skip = start // tile, (start - others_from) // tile
    pair = pl.BlockSpec((2, tile, depth), lambda i, _: (0, i + skip, 0))
    flat = pl.BlockSpec((tile, depth), lambda i, _: (i + skip, 0))
    grid_spec = pltpu.PrefetchScalarGridSpec(
        num_scalar_prefetch=1,
        grid=(rows // tile,),
        in_specs=[
            pl.BlockSpec((1, tile, depth), lambda i, side: (side[0], i + shift, 0)),
            flat,
        ]
        + [pair if other.ndim == 3 else flat for other in others]
        + [pl.BlockSpec(weight.shape, lambda i, _: (0, 0)) for weight in weights],
        out_specs=[pl.BlockSpec((tile, width), lambda i, _: (i, 0))] * 2,
    )
    return pl.pallas_call(
        functools.partial(mix_kernel, len(weights)),
        grid_spec=grid_spec,
        out_shape=[jax.ShapeDtypeStruct((rows, width), jnp.bfloat16)] * 2,
        compiler_params=pltpu.CompilerParams(vmem_limit_bytes=VMEM),
        cost_estimate=pl.CostEstimate(
            flops=2 * rows * depth * 2 * width * len(weights),
            bytes_accessed=2 * rows * (len(weights) * depth + 2 * width),
            transcendentals=0,
        ),
    )((lax.axis_index("mp") % 2).reshape(1), halves, near, *others, *weights)


def agg_kernel(where, source_rows, pull_count, side, bias, adj, *rest):
    *sources, out, table, tiles_of, rows_of, table_sems, adj_sems, out_sems = rest
    target_blocks, tiles = adj.shape[:2]
    last = 2 * target_blocks
    pulled_blocks = table.shape[0] // BLOCK - last
    slots = pulled_blocks // pull_count.shape[0]
    groups = target_blocks // UNROLL

    def tiles_in(group):
        here = pl.ds(group * UNROLL, UNROLL)
        return pltpu.make_async_copy(adj.at[here], tiles_of.at[here], adj_sems.at[group])

    def rows_out(group):
        here = pl.ds(pl.multiple_of(group * UNROLL * BLOCK, BLOCK), UNROLL * BLOCK)
        return pltpu.make_async_copy(rows_of.at[here], out.at[here], out_sems.at[group])

    copies = []
    for i, (which, rows, row) in enumerate(where):
        copies.append(pltpu.make_async_copy(sources[which], table.at[pl.ds(row, rows)], table_sems.at[i]))
        copies[-1].start()
    for group in range(groups):
        tiles_in(group).start()
    for copy in copies:
        copy.wait()

    def clear(slot, carry):
        @pl.when(slot % slots >= pull_count[slot // slots])
        def _():
            row = pl.multiple_of((last + (slot ^ (side[0] * (pulled_blocks // 2)))) * BLOCK, BLOCK)
            table[pl.ds(row, BLOCK), :] = jnp.zeros((BLOCK, table.shape[1]), table.dtype)

        return carry

    lax.fori_loop(0, pulled_blocks, clear, 0)

    def some(group, carry):
        tiles_in(group).wait()
        for u in range(UNROLL):
            t = group * UNROLL + u
            lhs = jnp.concatenate([tiles_of[t, k] for k in range(tiles)], axis=1)
            picks = []
            for k in range(tiles):
                row = pl.multiple_of(source_rows[t * tiles + k], BLOCK)
                picks.append(table[pl.ds(row, BLOCK), :])
            total = jnp.dot(lhs, jnp.concatenate(picks, axis=0), preferred_element_type=jnp.float32)
            row = pl.multiple_of(t * BLOCK, BLOCK)
            rows_of[pl.ds(row, BLOCK), :] = jnp.maximum(total + bias[...], 0.0).astype(rows_of.dtype)
        rows_out(group).start()
        return carry

    lax.fori_loop(0, groups, some, 0)
    for group in range(groups):
        rows_out(group).wait()


def aggregate(source_rows, pull_count, adj_values, bias, tables):
    target_blocks, tiles = adj_values.shape[:2]
    width = bias.shape[0]
    where, total_rows = [], 0
    for i, array in enumerate(tables):
        where.append((i, array.shape[0], total_rows))
        total_rows += array.shape[0]
    groups = target_blocks // UNROLL
    grid_spec = pltpu.PrefetchScalarGridSpec(
        num_scalar_prefetch=3,
        grid=(1,),
        in_specs=[pl.BlockSpec((1, width), lambda i, *_: (0, 0))]
        + [pl.BlockSpec(memory_space=pl.ANY)] * (1 + len(tables)),
        out_specs=pl.BlockSpec(memory_space=pl.ANY),
        scratch_shapes=[
            pltpu.VMEM((total_rows, width), jnp.bfloat16),
            pltpu.VMEM(adj_values.shape, jnp.bfloat16),
            pltpu.VMEM((target_blocks * BLOCK, width), jnp.bfloat16),
            pltpu.SemaphoreType.DMA((len(where),)),
            pltpu.SemaphoreType.DMA((groups,)),
            pltpu.SemaphoreType.DMA((groups,)),
        ],
    )
    return pl.pallas_call(
        functools.partial(agg_kernel, where),
        grid_spec=grid_spec,
        out_shape=jax.ShapeDtypeStruct((target_blocks * BLOCK, width), jnp.bfloat16),
        compiler_params=pltpu.CompilerParams(vmem_limit_bytes=SUM_VMEM),
        cost_estimate=pl.CostEstimate(
            flops=2 * target_blocks * tiles * BLOCK * BLOCK * width,
            bytes_accessed=2 * (target_blocks * tiles * BLOCK * BLOCK + total_rows * width),
            transcendentals=0,
        ),
    )(source_rows, pull_count, (lax.axis_index("mp") % 2).reshape(1), bias.reshape(1, -1), adj_values, *tables)


def far_weight(weight):
    mp_count = lax.axis_size("mp")
    chip = lax.axis_index("mp") // 2
    both = 2 * weight.shape[1] // mp_count
    pairs = []
    for d in range(mp_count // 2):
        pair = lax.dynamic_slice_in_dim(weight, (chip ^ d) * both, both, axis=1)
        pairs.append(swap(pair, "mp", 2 * d) if d else pair)
    return pairs


def all_weight(*pairs):
    return [part for pair in pairs for part in (pair, swap(pair, "mp", 1))]


def transfers(low, features, history, adj_sources, pull_list, weight, go):
    depth = features.shape[1]
    halves = features.reshape(2, -1, depth)
    rows = halves.shape[1]
    cut = rows * FIRST // 16
    send = [(0, cut), (cut, rows)]

    weights = far_weight(weight)
    mine = side_of(halves, 0)
    place = 1 - lax.axis_index("mp") % 2
    near = []
    for start, end in send:
        part = lax.dynamic_slice(halves, (place, start, 0), (1, end - start, depth))[0]
        near.append(swap(part, "mp", 1))
    wanted = lax.all_to_all(after(pull_list, near[0]), "dp", split_axis=0, concat_axis=0, tiled=True)
    sent = mine
    crossed = [far(jnp.stack([sent[start:end], part])) for part, (start, end) in zip(near, send)]

    def spread_weight(adj_sources, *pairs):
        blocks = adj_sources.reshape(-1)
        side = lax.axis_index("mp") % 2
        last = 2 * features.shape[0] // BLOCK
        pulled_blocks = pull_list.size
        half = jnp.where(blocks < last, last // 2, pulled_blocks) // 2
        moved = jnp.where(blocks < last, blocks ^ half, ((blocks - last) ^ half) + last)
        return jnp.where(side == 0, blocks, moved) * BLOCK, all_weight(*pairs)

    source_rows, columns = sealed(spread_weight, go, adj_sources, after(weights[0], near[0]), *weights[1:])
    picked = history.reshape(-1, BLOCK, depth)[after(wanted, *weights)]
    pulled = lax.all_to_all(picked, "dp", split_axis=0, concat_axis=0, tiled=True)

    def to_partner(here, beside):
        return (swap(here, "dp", low) if low else here), swap_both(beside, low, 1)

    def settle(columns, foreign, beside):
        near = swap(side_of(foreign, 1), "mp", 1)
        others = far(jnp.stack([side_of(foreign, 0), near]))
        here, foreign_beside = mix(foreign, near, others, columns, 0, near.shape[0])
        beside = swap(after(beside, *others), "mp", 1)
        return here, [beside, swap(after(foreign_beside, beside), "mp", 1)]

    first, rest = crossed
    own, beside = mix(halves, near[0], first, columns, 0, cut)
    moved = to_partner(own, beside)
    own_near = swap(beside, "mp", 1)
    rest[0] = after(rest[0], own, own_near)
    own_rest, beside = mix(halves, near[1], rest, columns, cut, rows, cut)
    moved_rest = to_partner(own_rest, beside)
    foreign = after(pulled, own_rest).reshape(2, -1, depth)
    foreign, swapped = sealed(settle, go, columns, foreign, beside)
    table = [own, own_rest, own_near, swapped[0], moved[0], moved_rest[0], moved[1], moved_rest[1]]
    return source_rows, [*table, foreign, swapped[-1]]


def per_device(
    features, history, adj_values, adj_sources, pull_list, pull_count, partner_mask, weight, bias
):
    mask = partner_mask[0]
    mask_bits = lax.axis_size("dp").bit_length() - 1
    done = min(DIGIT_BITS, mask_bits)
    first = 1 if mask_bits <= DIGIT_BITS else 0
    source_rows, tables = lax.switch(
        mask % (1 << done) - first,
        [functools.partial(transfers, low) for low in range(first, 1 << done)],
        features,
        history,
        adj_sources,
        pull_list[0],
        weight,
        mask > 0,
    )
    own, partner, pulled = tables[:4], tables[4:8], tables[8:]
    while done < mask_bits:
        bits = min(DIGIT_BITS, mask_bits - done)
        moves = [
            functools.partial(lambda d, *values: [swap(value, "dp", d) for value in values], digit << done)
            for digit in range(1, 1 << bits)
        ]
        partner = lax.switch((mask >> done) % (1 << bits), [lambda *values: list(values)] + moves, *partner)
        done += bits
    return aggregate(source_rows, pull_count[0], adj_values, bias, [*own, *partner, *pulled])


def solution(mesh):
    in_specs = (
        P("dp", "mp"),
        P("dp", "mp"),
        P("dp", None, None, None),
        P("dp", None),
        P("dp", None, None),
        P("dp", None),
        P(),
        P("mp", None),
        P("mp"),
    )
    out_specs = P("dp", "mp")
    return jax.shard_map(
        per_device, mesh=mesh, in_specs=in_specs, out_specs=out_specs, check_vma=False
    )
```
